32 devices in a mesh: dp: 8 (over y, x, core), tensor: 4 (over z).
Axes of the slice: x: 2, y: 2, z: 4, core: 2. Of those that a mesh axis runs over, the one named last changes fastest.
Arguments:
- tokens: bfloat16 [16384, 768], P(('dp', 'tensor')), may hold values from -6 to 6
- cotangent: bfloat16 [16384, 768], P(('dp', 'tensor')), may hold values from -6 to 6
- w_qkv: float32 [3, 768, 768], P(None, 'dp', 'tensor'), may hold values from -0.21875 to 0.21875
- w_out: float32 [768, 768], P('tensor', 'dp'), may hold values from -1.75 to 1.75
- w_up: float32 [768, 3072], P('dp', 'tensor'), may hold values from -0.21875 to 0.21875
- w_down: float32 [3072, 768], P('tensor', 'dp'), may hold values from -0.109375 to 0.109375
- vectors: float32 [9216], replicated, may hold values from -0.9 to 1.5, as said below
- m_qkv: float32 [3, 768, 768], P(None, 'dp', 'tensor'), may hold values from -80 to 80
- v_qkv: float32 [3, 768, 768], P(None, 'dp', 'tensor'), may hold values from 16.384 to 65.536
- m_out: float32 [768, 768], P('tensor', 'dp'), may hold values from -24 to 24
- v_out: float32 [768, 768], P('tensor', 'dp'), may hold values from 1.47456 to 5.89824
- m_up: float32 [768, 3072], P('dp', 'tensor'), may hold values from -24 to 24
- v_up: float32 [768, 3072], P('dp', 'tensor'), may hold values from 1.47456 to 5.89824
- m_down: float32 [3072, 768], P('tensor', 'dp'), may hold values from -56 to 56
- v_down: float32 [3072, 768], P('tensor', 'dp'), may hold values from 6.88128 to 27.8528
- m_vec: float32 [9216], replicated, may hold values from -80 to 80
- v_vec: float32 [9216], replicated, may hold values from 16.384 to 65.536
Outputs:
- output: bfloat16 [16384, 768], P(('dp', 'tensor'))
- grad_tokens: float32 [16384, 768], P(('dp', 'tensor'))
- qkv_mean: float32 [3, 768, 768], P(None, 'dp', 'tensor')
- qkv_square: float32 [3, 768, 768], P(None, 'dp', 'tensor')
- qkv_weight: float32 [3, 768, 768], P(None, 'dp', 'tensor')
- out_mean: float32 [768, 768], P('tensor', 'dp')
- out_square: float32 [768, 768], P('tensor', 'dp')
- out_weight: float32 [768, 768], P('tensor', 'dp')
- up_mean: float32 [768, 3072], P('dp', 'tensor')
- up_square: float32 [768, 3072], P('dp', 'tensor')
- up_weight: float32 [768, 3072], P('dp', 'tensor')
- down_mean: float32 [3072, 768], P('tensor', 'dp')
- down_square: float32 [3072, 768], P('tensor', 'dp')
- down_weight: float32 [3072, 768], P('tensor', 'dp')
- vec_mean: float32 [9216], replicated
- vec_square: float32 [9216], replicated
- vec_values: float32 [9216], replicated
The draws below stay inside these ranges and needn't reach their ends.
Inputs may be any that keep to these rules, and one draw needn't show every extreme that they name: `vectors`: entries 0 to 767 and 1536 to 2303 are norm gains between 0.5 and 1.5; all others are shifts and biases.
All inputs are finite; a program needn't handle non-finite values.
Results may differ from the reference program's by a relative error of at most 0.017.
Values may be sent and summed in bfloat16 or wider, within the bound.
A program may use at most 128 MiB of HBM per device.

```python
import math
import jax
import jax.numpy as jnp
from jax import lax

D = 768
HEADS = 12
HEAD = 64
FF = 3072
LENGTH = 1024
TOK_DEV = 512
STEP = 10
TOKENS = 16384
N_TENSOR = 4


def draw_vectors(key, part):
    key = jax.random.fold_in(key, 11)
    gain_key, shift_key = jax.random.split(key)
    gain_rows = jax.random.uniform(gain_key, (2, D), jnp.float32, 0.5, 1.5)
    shift_rows = 0.3 * jnp.clip(jax.random.normal(shift_key, (6 * D + FF,), jnp.float32), -3.0, 3.0)
    return jnp.concatenate([gain_rows[0], shift_rows[0:D], gain_rows[1], shift_rows[D:]])


def levels(rng, dims, cuts, low, top_value):
    def one(dim, parts):
        steps = jax.random.uniform(jax.random.fold_in(jax.random.fold_in(rng, 6), dim), (parts,), jnp.float32, low / len(cuts), top_value / len(cuts))
        return jnp.repeat(jnp.exp(steps), dims[dim] // parts).reshape((-1,) + (1,) * (len(dims) - dim - 1))

    factor_of = one(*cuts[0])
    for cut in cuts[1:]:
        factor_of = factor_of * one(*cut)
    return factor_of


def gaussian(key, dims, scale, most, cuts=(), kind=jnp.bfloat16):
    values = jax.random.normal(key, dims, jnp.float32) * scale
    if len(cuts) > 0:
        values = levels(key, dims, cuts, -0.22, 0.18) * values
    return jnp.clip(values, min=-most, max=most).astype(kind)


def setup_inputs(seed: int = 0) -> dict:
    arg_keys = jax.random.split(jax.random.key(seed), 18)
    tokens = gaussian(arg_keys[0], (TOKENS, D), 1.0, 6.0, ((0, 32),))
    cotangent = gaussian(arg_keys[1], (TOKENS, D), 1.0, 6.0, ((0, 32),))
    w_qkv = gaussian(arg_keys[2], (3, D, D), D ** -0.5, 0.21875, ((1, 8), (2, 4)), jnp.float32)
    w_out = gaussian(arg_keys[3], (D, D), (D // 64) ** -0.5, 1.75, ((0, 4), (1, 8)), jnp.float32)
    w_up = gaussian(arg_keys[4], (D, FF), D ** -0.5, 0.21875, ((0, 8), (1, 4)), jnp.float32)
    w_down = gaussian(arg_keys[5], (FF, D), FF ** -0.5, 0.109375, ((0, 4), (1, 8)), jnp.float32)
    vectors = draw_vectors(jax.random.fold_in(arg_keys[17], 71), 0)
    m_qkv = gaussian(arg_keys[7], (3, D, D), (0.11 * TOKENS ** 0.5), 80.0, ((1, 8), (2, 4)), jnp.float32)
    v_qkv = jnp.clip(jnp.exp(math.log(65.536) - 1.3862944 * jax.random.uniform(arg_keys[8], (3, D, D), jnp.float32) ** levels(arg_keys[8], (3, D, D), ((1, 8), (2, 4)), -0.2, 0.2)), 16.384, 65.536)
    m_out = gaussian(arg_keys[9], (D, D), (0.033 * TOKENS ** 0.5), 24.0, ((0, 4), (1, 8)), jnp.float32)
    v_out = jnp.clip(jnp.exp(math.log(5.89824) - 1.3862944 * jax.random.uniform(arg_keys[10], (D, D), jnp.float32) ** levels(arg_keys[10], (D, D), ((0, 4), (1, 8)), -0.2, 0.2)), 1.47456, 5.89824)
    m_up = gaussian(arg_keys[11], (D, FF), (0.033 * TOKENS ** 0.5), 24.0, ((0, 8), (1, 4)), jnp.float32)
    v_up = jnp.clip(jnp.exp(math.log(5.89824) - 1.3862944 * jax.random.uniform(arg_keys[12], (D, FF), jnp.float32) ** levels(arg_keys[12], (D, FF), ((0, 8), (1, 4)), -0.2, 0.2)), 1.47456, 5.89824)
    m_down = gaussian(arg_keys[13], (FF, D), (0.072 * TOKENS ** 0.5), 56.0, ((0, 4), (1, 8)), jnp.float32)
    v_down = jnp.clip(jnp.exp(math.log(27.8528) - 1.39812884 * jax.random.uniform(arg_keys[14], (FF, D), jnp.float32) ** levels(arg_keys[14], (FF, D), ((0, 4), (1, 8)), -0.2, 0.2)), 6.88128, 27.8528)
    m_vec = gaussian(arg_keys[15], (8 * D + FF,), (0.11 * TOKENS ** 0.5), 80.0, (), jnp.float32)
    v_vec = jnp.clip(jnp.exp(jax.random.uniform(arg_keys[16], (8 * D + FF,), jnp.float32, math.log(16.384), math.log(65.536))), 16.384, 65.536)
    return {"tokens": tokens, "cotangent": cotangent, "w_qkv": w_qkv, "w_out": w_out, "w_up": w_up, "w_down": w_down, "vectors": vectors, "m_qkv": m_qkv, "v_qkv": v_qkv, "m_out": m_out, "v_out": v_out, "m_up": m_up, "v_up": v_up, "m_down": m_down, "v_down": v_down, "m_vec": m_vec, "v_vec": v_vec}


@jax.custom_vjp
def low(v):
    return lax.optimization_barrier(v.astype(jnp.bfloat16)).astype(jnp.float32)

@jax.custom_vjp
def low_back(v):
    return v

def low_keep(v):
    return (low(v), None)

def low_pass(kept, grad):
    return (grad,)

def back_keep(v):
    return (v, None)

def back_low(kept, grad):
    return (low(grad),)
low.defvjp(low_keep, low_pass)
low_back.defvjp(back_keep, back_low)
EPSILON = 1e-05
BETA_ONE = 0.9
BETA_TWO = 0.999
ADAM_EPSILON = 1e-08
WEIGHT_DECAY = 0.1
VECTOR_RATE = 0.3
MASKED = -1e+30
PRECISE = lax.Precision.HIGHEST

def matmul(left, right):
    return jnp.dot(left, right, precision=PRECISE)

def layer_norm(values, gain_row, shift_row):
    row_mean = lax.optimization_barrier(jnp.mean(values, axis=-1, keepdims=True))
    centred = values - row_mean
    spread = lax.optimization_barrier(jnp.mean(centred * centred, axis=-1, keepdims=True))
    return centred * lax.rsqrt(spread + EPSILON) * gain_row + shift_row

def attend(inputs):
    queries, key_rows, values = inputs
    scores = jnp.einsum('qhd,khd->hqk', queries, key_rows, precision=PRECISE)
    scores = low_back(scores * HEAD ** (-0.5))
    positions = jnp.arange(LENGTH)
    causal = positions[:, None] >= positions[None, :]
    scores = jnp.where(causal[None], scores, MASKED)
    softmax_rows = low(jax.nn.softmax(scores, axis=-1))
    return jnp.einsum('hqk,khd->qhd', softmax_rows, values, precision=PRECISE)

def block_forward(token_rows, w_qkv, w_out, w_up, w_down, vectors):
    normed = low(layer_norm(token_rows, vectors[0:D], vectors[D:2 * D]))
    qkv_low = low(w_qkv)
    queries = low(low_back(matmul(normed, qkv_low[0]) + vectors[6 * D:7 * D]))
    key_rows = low(low_back(matmul(normed, qkv_low[1])))
    values = low(low_back(matmul(normed, qkv_low[2]) + vectors[7 * D:8 * D]))
    row_total = token_rows.shape[0]
    head_shape = (row_total // LENGTH, LENGTH, HEADS, HEAD)
    attended = lax.map(jax.checkpoint(attend), (queries.reshape(head_shape), key_rows.reshape(head_shape), values.reshape(head_shape)))
    attended = low(low_back(attended.reshape(row_total, D)))
    hidden = token_rows + low_back(matmul(attended, low(w_out))) + vectors[4 * D:5 * D]
    normed_two = low(layer_norm(hidden, vectors[2 * D:3 * D], vectors[3 * D:4 * D]))
    pre_act = low_back(matmul(normed_two, low(w_up)) + vectors[8 * D:])
    active = low(jax.nn.gelu(pre_act))
    return hidden + low_back(matmul(active, low(w_down))) + vectors[5 * D:6 * D]

def adam_update(weight, gradient, first_moment, second_moment, step_rate, decay_rate):
    first_new = BETA_ONE * first_moment + (1.0 - BETA_ONE) * gradient
    second_new = BETA_TWO * second_moment + (1.0 - BETA_TWO) * gradient * gradient
    first_hat = first_new / (1.0 - BETA_ONE ** STEP)
    second_hat = second_new / (1.0 - BETA_TWO ** STEP)
    weight_new = weight - step_rate * (first_hat / (jnp.sqrt(second_hat) + ADAM_EPSILON) + decay_rate * weight)
    return (first_new, second_new, weight_new)

def reference(tokens, cotangent, w_qkv, w_out, w_up, w_down, vectors, m_qkv, v_qkv, m_out, v_out, m_up, v_up, m_down, v_down, m_vec, v_vec):
    params = (w_qkv, w_out, w_up, w_down, vectors)
    group_rows = TOK_DEV * N_TENSOR
    group_count = TOKENS // group_rows
    token_groups = tokens.astype(jnp.float32).reshape(group_count, group_rows, D)
    cot_groups = cotangent.astype(jnp.float32).reshape(group_count, group_rows, D)

    def one_group(totals, inputs):
        token_rows, cot_rows = inputs
        result, pullback = jax.vjp(block_forward, token_rows, *params)
        gradients = pullback(cot_rows)
        totals = tuple((total + extra for total, extra in zip(totals, gradients[1:])))
        return (totals, (result.astype(jnp.bfloat16), gradients[0]))
    zero_sums = tuple((jnp.zeros_like(param) for param in params))
    totals, (outputs, grad_rows) = lax.scan(one_group, zero_sums, (token_groups, cot_groups))
    grad_qkv, grad_out, grad_up, grad_down, grad_vec = totals
    qkv_new = adam_update(w_qkv, grad_qkv, m_qkv, v_qkv, D ** (-0.5), WEIGHT_DECAY)
    out_new = adam_update(w_out, grad_out, m_out, v_out, (D // 64) ** (-0.5), WEIGHT_DECAY)
    up_new = adam_update(w_up, grad_up, m_up, v_up, D ** (-0.5), WEIGHT_DECAY)
    down_new = adam_update(w_down, grad_down, m_down, v_down, FF ** (-0.5), WEIGHT_DECAY)
    vec_new = adam_update(vectors, grad_vec, m_vec, v_vec, VECTOR_RATE, 0.0)
    return (outputs.reshape(TOKENS, D), grad_rows.reshape(TOKENS, D), qkv_new[0], qkv_new[1], qkv_new[2], out_new[0], out_new[1], out_new[2], up_new[0], up_new[1], up_new[2], down_new[0], down_new[1], down_new[2], vec_new[0], vec_new[1], vec_new[2])
```

```python
import jax
import jax.numpy as jnp
from jax import lax
from jax.experimental import pallas as pl
from jax.experimental.pallas import tpu as pltpu
from jax.sharding import PartitionSpec as P

D = 768
HEAD = 64
FF = 3072
LENGTH = 1024
STEP = 10


EPSILON = 1e-05
BETA_ONE = 0.9
BETA_TWO = 0.999
ADAM_EPSILON = 1e-08
WEIGHT_DECAY = 0.1
VECTOR_RATE = 0.3
MASKED = -1e30


def layer_norm(values, gain_row, shift_row):
    row_mean = jnp.mean(values, axis=-1, keepdims=True)
    centred = values - row_mean
    spread = jnp.mean(centred * centred, axis=-1, keepdims=True)
    return centred * lax.rsqrt(spread + EPSILON) * gain_row + shift_row


def adam_update(weight, gradient, first_moment, second_moment, step_rate, decay_rate):
    first_new = BETA_ONE * first_moment + (1.0 - BETA_ONE) * gradient
    second_new = BETA_TWO * second_moment + (1.0 - BETA_TWO) * gradient * gradient
    first_hat = first_new / (1.0 - BETA_ONE**STEP)
    second_hat = second_new / (1.0 - BETA_TWO**STEP)
    weight_new = weight - step_rate * (
        first_hat / (jnp.sqrt(second_hat) + ADAM_EPSILON) + decay_rate * weight
    )
    return (first_new, second_new, weight_new)


F32 = jnp.float32
BF16 = jnp.bfloat16
BLOCK = 256


def contract(left, right, left_dim, right_dim):
    return lax.dot_general(
        left, right, (((left_dim,), (right_dim,)), ((), ())), preferred_element_type=F32
    )


def block_mask(scores, first_query):
    keys = lax.broadcasted_iota(jnp.int32, scores.shape, 0)
    queries = first_query + lax.broadcasted_iota(jnp.int32, scores.shape, 1)
    return jnp.where(keys <= queries, scores, MASKED)


def forward_kernel(qkv_ref, out_ref, lse_ref):
    length = qkv_ref.shape[-1]
    scale = HEAD ** (-0.5)
    for first in range(0, length, BLOCK):
        count = first + BLOCK
        rows = slice(first, count)
        scores = contract(qkv_ref[0, 1, 0, :, :count], qkv_ref[0, 0, 0, :, rows], 0, 0) * scale
        scores = block_mask(scores, first)
        largest = jnp.max(scores, axis=0, keepdims=True)
        weights = jnp.exp(scores - largest)
        total = jnp.sum(weights, axis=0, keepdims=True)
        probs = (weights * (1.0 / total)).astype(BF16)
        out_ref[0, 0, :, rows] = contract(qkv_ref[0, 2, 0, :, :count], probs, 1, 0).astype(BF16)
        lse_ref[0, 0, :, rows] = largest + jnp.log(total)


def backward_kernel(qkv_ref, lse_ref, grad_ref, out_ref, key_sum, value_sum):
    length = qkv_ref.shape[-1]
    scale = HEAD ** (-0.5)
    key_sum[...] = jnp.zeros_like(key_sum)
    value_sum[...] = jnp.zeros_like(value_sum)
    for first in range(0, length, BLOCK):
        count = first + BLOCK
        rows = slice(first, count)
        queries = qkv_ref[0, 0, 0, :, rows]
        keys = qkv_ref[0, 1, 0, :, :count]
        grad_out = grad_ref[0, 0, :, rows]
        scores = block_mask(contract(keys, queries, 0, 0) * scale, first)
        probs = jnp.exp(scores - lse_ref[0, 0, :, rows])
        grad_probs = contract(qkv_ref[0, 2, 0, :, :count], grad_out, 0, 0)
        inner = jnp.sum(probs * grad_probs, axis=0, keepdims=True)
        grad_scores = (probs * (grad_probs - inner)).astype(BF16)
        out_ref[0, 0, 0, :, rows] = (contract(keys, grad_scores, 1, 0) * scale).astype(BF16)
        key_sum[:, :count] += contract(queries, grad_scores, 1, 1)
        value_sum[:, :count] += contract(grad_out, probs.astype(BF16), 1, 1)
    out_ref[0, 1, 0] = (key_sum[...] * scale).astype(BF16)
    out_ref[0, 2, 0] = value_sum[...].astype(BF16)


def attend_forward(qkv):
    groups, _, heads, width, length = qkv.shape
    return pl.pallas_call(
        forward_kernel,
        grid=(groups, heads),
        in_specs=[pl.BlockSpec((1, 3, 1, width, length), lambda g, h: (g, 0, h, 0, 0))],
        out_specs=[
            pl.BlockSpec((1, 1, width, length), lambda g, h: (g, h, 0, 0)),
            pl.BlockSpec((1, 1, 1, length), lambda g, h: (g, h, 0, 0)),
        ],
        out_shape=[
            jax.ShapeDtypeStruct((groups, heads, width, length), BF16),
            jax.ShapeDtypeStruct((groups, heads, 1, length), F32),
        ],
        compiler_params=pltpu.CompilerParams(vmem_limit_bytes=32 * 1024 * 1024),
        cost_estimate=pl.CostEstimate(
            flops=4 * groups * heads * length * length * width,
            bytes_accessed=8 * groups * heads * length * width,
            transcendentals=groups * heads * length * length,
        ),
    )(qkv)


def attend_backward(qkv, log_sums, grad_out):
    groups, _, heads, width, length = qkv.shape
    return pl.pallas_call(
        backward_kernel,
        grid=(groups, heads),
        in_specs=[
            pl.BlockSpec((1, 3, 1, width, length), lambda g, h: (g, 0, h, 0, 0)),
            pl.BlockSpec((1, 1, 1, length), lambda g, h: (g, h, 0, 0)),
            pl.BlockSpec((1, 1, width, length), lambda g, h: (g, h, 0, 0)),
        ],
        out_specs=pl.BlockSpec((1, 3, 1, width, length), lambda g, h: (g, 0, h, 0, 0)),
        out_shape=jax.ShapeDtypeStruct(qkv.shape, BF16),
        scratch_shapes=[pltpu.VMEM((width, length), F32), pltpu.VMEM((width, length), F32)],
        compiler_params=pltpu.CompilerParams(vmem_limit_bytes=32 * 1024 * 1024),
        cost_estimate=pl.CostEstimate(
            flops=10 * groups * heads * length * length * width,
            bytes_accessed=14 * groups * heads * length * width,
            transcendentals=groups * heads * length * length,
        ),
    )(qkv, log_sums, grad_out)


def swap(values, axis_name, distance):
    size = lax.axis_size(axis_name)
    return lax.ppermute(values, axis_name, [(i, i ^ distance) for i in range(size)])


def bit_of(axis_name, bit):
    return lax.rem(lax.axis_index(axis_name) // (1 << bit), 2)


def gather_data(values, order):
    bits = len(order)
    blocks, rows, columns = values.shape
    values = values.reshape((blocks,) + (1,) * bits + (rows, columns))
    for bit in order:
        other = swap(values, "dp", 1 << bit)
        low = bit_of("dp", bit) == 0
        values = jnp.concatenate(
            [jnp.where(low, values, other), jnp.where(low, other, values)], axis=bits - bit
        )
    return values.reshape(blocks, rows << bits, columns)


def scatter_data(values, order):
    bits = len(order)
    blocks, rows, columns = values.shape
    values = values.reshape((blocks,) + (2,) * bits + (rows >> bits, columns))
    for bit in order:
        mine = bit_of("dp", bit)
        axis = bits - bit
        other = swap(
            lax.dynamic_index_in_dim(values, 1 - mine, axis, keepdims=True), "dp", 1 << bit
        )
        kept = lax.dynamic_index_in_dim(values, mine, axis, keepdims=True)
        values = (kept.astype(F32) + other.astype(F32)).astype(BF16)
    return values.reshape(blocks, rows >> bits, columns)


def gather_blocks(shard, distances):
    return jnp.stack([shard if d == 0 else swap(shard, "tensor", d) for d in distances])


def scatter_blocks(values, distances):
    total = values[0].astype(F32)
    for index, distance in enumerate(distances):
        if distance:
            total = total + swap(values[index], "tensor", distance).astype(F32)
    return total


def reduce_all(values):
    for axis_name in ("dp", "tensor"):
        distance = 1
        while distance < lax.axis_size(axis_name):
            values = values + swap(values, axis_name, distance)
            distance *= 2
    return values


def on_device(
    tokens,
    cotangent,
    w_qkv,
    w_out,
    w_up,
    w_down,
    vectors,
    m_qkv,
    v_qkv,
    m_out,
    v_out,
    m_up,
    v_up,
    m_down,
    v_down,
    m_vec,
    v_vec,
):
    width = tokens.shape[1]
    rows = tokens.shape[0]
    head_cols = w_qkv.shape[2]
    unit_cols = w_up.shape[1]
    own_rows = w_up.shape[0]
    n_tensor = lax.axis_size("tensor")
    bits = lax.axis_size("dp").bit_length() - 1
    outer = list(range(1, bits))
    gather_one, gather_two = outer + [0], outer[::-1] + [0]
    scatter_one, scatter_two = [0] + outer, [0] + outer[::-1]
    rank = lax.axis_index("tensor")
    every = list(range(n_tensor))
    owned = every[::2]

    def vector(index):
        return vectors[index * width : (index + 1) * width]

    def ranked(first, count, distances):
        return jnp.stack(
            [
                lax.dynamic_slice_in_dim(vectors, first + (rank ^ d) * count, count)
                for d in distances
            ]
        )

    token_rows = tokens.astype(F32)
    cot_rows = cotangent.astype(F32)
    normed_one, norm_one_pull = jax.vjp(layer_norm, token_rows, vector(0), vector(1))
    normed_one = normed_one.astype(BF16)
    normed_other = swap(normed_one, "tensor", 1)
    half = lax.rem(rank, 2)
    first_half = half == 0
    normed_pair = jnp.concatenate(
        [
            jnp.where(first_half, normed_one, normed_other),
            jnp.where(first_half, normed_other, normed_one),
        ]
    )

    def exchange(values, axis):
        kept = lax.dynamic_slice_in_dim(values, half * rows, rows, axis)
        given = lax.dynamic_slice_in_dim(values, (1 - half) * rows, rows, axis)
        return kept, swap(given, "tensor", 1)

    qkv_shard = w_qkv.astype(BF16).transpose(1, 0, 2).reshape(own_rows, 3 * head_cols)
    qkv_full = gather_data(gather_blocks(qkv_shard, owned), gather_one)
    out_full = gather_data(gather_blocks(w_out.astype(BF16).T, every), gather_two)
    up_full = gather_data(gather_blocks(w_up.astype(BF16), every), gather_one)
    down_full = gather_data(gather_blocks(w_down.astype(BF16).T, every), gather_two)

    query_bias = ranked(6 * width, head_cols, owned)
    value_bias = ranked(7 * width, head_cols, owned)
    biases = jnp.concatenate([query_bias, jnp.zeros_like(query_bias), value_bias], axis=1)
    projected = jnp.einsum("jde,nd->jen", qkv_full, normed_pair, preferred_element_type=F32)
    projected = (projected + biases[:, :, None]).astype(BF16)
    heads = head_cols // HEAD
    split = projected.reshape(len(owned), 3, heads, HEAD, 2 * rows)
    attended, log_sums = attend_forward(split)
    attended = attended.reshape(len(owned), head_cols, 2 * rows)
    attended_own, attended_got = exchange(attended, 2)
    attended_all = jnp.stack([attended_own, attended_got], axis=1).reshape(
        n_tensor, head_cols, rows
    )
    branch = jnp.einsum("jen,jde->nd", attended_all, out_full, preferred_element_type=F32)
    hidden = token_rows + branch + vector(4)
    normed_two, norm_two_pull = jax.vjp(layer_norm, hidden, vector(2), vector(3))
    normed_two = normed_two.astype(BF16)
    up_bias = ranked(8 * width, unit_cols, every)
    pre_act = (
        jnp.einsum("nd,jdf->jnf", normed_two, up_full, preferred_element_type=F32)
        + up_bias[:, None, :]
    )
    active, gelu_pull = jax.vjp(jax.nn.gelu, pre_act)
    active = active.astype(BF16)
    output = (
        hidden
        + jnp.einsum("jnf,jdf->nd", active, down_full, preferred_element_type=F32)
        + vector(5)
    )
    grad_active = jnp.einsum("nd,jdf->jnf", cotangent, down_full, preferred_element_type=F32)
    grad_pre = gelu_pull(grad_active)[0].astype(BF16)
    grad_down = jnp.einsum(
        "nd,jnf->jdf", cotangent, active, preferred_element_type=F32
    ).astype(BF16)
    grad_up = jnp.einsum("nd,jnf->jdf", normed_two, grad_pre, preferred_element_type=F32).astype(
        BF16
    )
    grad_normed_two = jnp.einsum("jnf,jdf->nd", grad_pre, up_full, preferred_element_type=F32)
    up_sums = jnp.sum(grad_pre.astype(F32), axis=1)
    grad_from_norm, grad_gain_two, grad_shift_two = norm_two_pull(grad_normed_two)
    grad_hidden = cot_rows + grad_from_norm
    grad_low = grad_hidden.astype(BF16)
    grad_attended = jnp.einsum(
        "nd,jde->jen", grad_low, out_full, preferred_element_type=F32
    ).astype(BF16)
    grad_pairs = grad_attended.reshape(len(owned), 2, head_cols, rows)
    grad_other = swap(grad_pairs[:, 1], "tensor", 1)
    grad_own = grad_pairs[:, 0]
    grad_heads = jnp.concatenate(
        [
            jnp.where(first_half, grad_own, grad_other),
            jnp.where(first_half, grad_other, grad_own),
        ],
        axis=2,
    )
    grad_out_w = jnp.einsum(
        "nd,jen->jde", grad_low, attended_all, preferred_element_type=F32
    ).astype(BF16)
    grad_down_own = scatter_blocks(scatter_data(grad_down, scatter_one), every)
    grad_up_own = scatter_blocks(scatter_data(grad_up, scatter_two), every)
    grad_out_own = scatter_blocks(scatter_data(grad_out_w, scatter_one), every)
    grad_split = attend_backward(
        split, log_sums, grad_heads.reshape(len(owned), heads, HEAD, 2 * rows)
    )
    grad_proj = grad_split.reshape(len(owned), 3 * head_cols, 2 * rows)
    grad_normed_pair = jnp.einsum(
        "jen,jde->nd", grad_proj, qkv_full, preferred_element_type=F32
    ).astype(BF16)
    kept, given = exchange(grad_normed_pair, 0)
    grad_normed_one = kept.astype(F32) + given.astype(F32)
    grad_qkv_w = jnp.einsum(
        "nd,jen->jde", normed_pair, grad_proj, preferred_element_type=F32
    ).astype(BF16)
    grad_qkv_own = scatter_blocks(scatter_data(grad_qkv_w, scatter_two), owned)
    grad_from_first, grad_gain_one, grad_shift_one = norm_one_pull(grad_normed_one)
    grad_tokens = grad_hidden + grad_from_first

    def placed(parts, count, full, distances):
        result = jnp.zeros((full,), F32)
        for index, distance in enumerate(distances):
            result = lax.dynamic_update_slice_in_dim(
                result, parts[index], (rank ^ distance) * count, 0
            )
        return result

    proj_sums = jnp.sum(grad_proj.astype(F32), axis=2)
    early = reduce_all(
        jnp.concatenate(
            [
                grad_gain_two,
                grad_shift_two,
                jnp.sum(grad_hidden, axis=0),
                jnp.sum(cot_rows, axis=0),
                placed(up_sums, unit_cols, n_tensor * unit_cols, every),
            ]
        )
    )
    late = reduce_all(
        jnp.concatenate(
            [
                grad_gain_one,
                grad_shift_one,
                placed(proj_sums[:, :head_cols], head_cols, width, owned),
                placed(proj_sums[:, 2 * head_cols :], head_cols, width, owned),
            ]
        )
    )
    vector_grad = jnp.concatenate(
        [
            late[: 2 * width],
            early[: 4 * width],
            late[2 * width :],
            early[4 * width :],
        ]
    )
    grad_qkv = grad_qkv_own.reshape(own_rows, 3, head_cols).transpose(1, 0, 2)
    qkv_new = adam_update(w_qkv, grad_qkv, m_qkv, v_qkv, D ** (-0.5), WEIGHT_DECAY)
    out_new = adam_update(w_out, grad_out_own.T, m_out, v_out, (D // 64) ** (-0.5), WEIGHT_DECAY)
    up_new = adam_update(w_up, grad_up_own, m_up, v_up, D ** (-0.5), WEIGHT_DECAY)
    down_new = adam_update(w_down, grad_down_own.T, m_down, v_down, FF ** (-0.5), WEIGHT_DECAY)
    vec_new = adam_update(vectors, vector_grad, m_vec, v_vec, VECTOR_RATE, 0.0)
    return (output.astype(BF16), grad_tokens, *qkv_new, *out_new, *up_new, *down_new, *vec_new)


def solution(mesh):
    return jax.shard_map(
        on_device,
        mesh=mesh,
        in_specs=(
            P(("dp", "tensor"), None),
            P(("dp", "tensor"), None),
            P(None, "dp", "tensor"),
            P("tensor", "dp"),
            P("dp", "tensor"),
            P("tensor", "dp"),
            P(),
            P(None, "dp", "tensor"),
            P(None, "dp", "tensor"),
            P("tensor", "dp"),
            P("tensor", "dp"),
            P("dp", "tensor"),
            P("dp", "tensor"),
            P("tensor", "dp"),
            P("tensor", "dp"),
            P(),
            P(),
        ),
        out_specs=(
            P(("dp", "tensor"), None),
            P(("dp", "tensor"), None),
            P(None, "dp", "tensor"),
            P(None, "dp", "tensor"),
            P(None, "dp", "tensor"),
            P("tensor", "dp"),
            P("tensor", "dp"),
            P("tensor", "dp"),
            P("dp", "tensor"),
            P("dp", "tensor"),
            P("dp", "tensor"),
            P("tensor", "dp"),
            P("tensor", "dp"),
            P("tensor", "dp"),
            P(),
            P(),
            P(),
        ),
        check_vma=False,
    )
```

```python
import jax
import jax.numpy as jnp
from jax import lax
from jax.experimental import pallas as pl
from jax.experimental.pallas import tpu as pltpu
from jax.experimental.layout import Layout, with_layout_constraint
from jax.sharding import PartitionSpec as P

D = 768
HEAD = 64
FF = 3072
LENGTH = 1024
STEP = 10


EPSILON = 1e-05
BETA_ONE = 0.9
BETA_TWO = 0.999
ADAM_EPSILON = 1e-08
WEIGHT_DECAY = 0.1
VECTOR_RATE = 0.3
MASKED = -1e30


def layer_norm(values, gain_row, shift_row):
    row_mean = jnp.mean(values, axis=-1, keepdims=True)
    centred = values - row_mean
    spread = jnp.mean(centred * centred, axis=-1, keepdims=True)
    return centred * lax.rsqrt(spread + EPSILON) * gain_row + shift_row


def adam_update(weight, gradient, first_moment, second_moment, step_rate, decay_rate):
    first_new = BETA_ONE * first_moment + (1.0 - BETA_ONE) * gradient
    second_new = BETA_TWO * second_moment + (1.0 - BETA_TWO) * gradient * gradient
    first_hat = first_new / (1.0 - BETA_ONE**STEP)
    second_hat = second_new / (1.0 - BETA_TWO**STEP)
    weight_new = weight - step_rate * (
        first_hat / (jnp.sqrt(second_hat) + ADAM_EPSILON) + decay_rate * weight
    )
    return (first_new, second_new, weight_new)


F32 = jnp.float32
BF16 = jnp.bfloat16
BLOCK = 256


def contract(left, right, left_dim, right_dim):
    return lax.dot_general(
        left, right, (((left_dim,), (right_dim,)), ((), ())), preferred_element_type=F32
    )


def block_mask(scores, first_query):
    keys = lax.broadcasted_iota(jnp.int32, scores.shape, 0)
    queries = first_query + lax.broadcasted_iota(jnp.int32, scores.shape, 1)
    return jnp.where(keys <= queries, scores, MASKED)


def forward_kernel(qkv_ref, out_ref, lse_ref):
    length = qkv_ref.shape[-1]
    scale = HEAD ** (-0.5)
    for first in range(0, length, BLOCK):
        count = first + BLOCK
        rows = slice(first, count)
        scores = contract(qkv_ref[0, 1, 0, :, :count], qkv_ref[0, 0, 0, :, rows], 0, 0) * scale
        scores = block_mask(scores, first)
        largest = jnp.max(scores, axis=0, keepdims=True)
        weights = jnp.exp(scores - largest)
        total = jnp.sum(weights, axis=0, keepdims=True)
        probs = (weights * (1.0 / total)).astype(BF16)
        out_ref[0, 0, :, rows] = contract(qkv_ref[0, 2, 0, :, :count], probs, 1, 0).astype(BF16)
        lse_ref[0, 0, :, rows] = largest + jnp.log(total)


def backward_kernel(qkv_ref, lse_ref, grad_ref, out_ref, key_sum, value_sum):
    length = qkv_ref.shape[-1]
    scale = HEAD ** (-0.5)
    key_sum[...] = jnp.zeros_like(key_sum)
    value_sum[...] = jnp.zeros_like(value_sum)
    for first in range(0, length, BLOCK):
        count = first + BLOCK
        rows = slice(first, count)
        queries = qkv_ref[0, 0, 0, :, rows]
        keys = qkv_ref[0, 1, 0, :, :count]
        grad_out = grad_ref[0, 0, :, rows]
        scores = block_mask(contract(keys, queries, 0, 0) * scale, first)
        probs = jnp.exp(scores - lse_ref[0, 0, :, rows])
        grad_probs = contract(qkv_ref[0, 2, 0, :, :count], grad_out, 0, 0)
        inner = jnp.sum(probs * grad_probs, axis=0, keepdims=True)
        grad_scores = (probs * (grad_probs - inner)).astype(BF16)
        out_ref[0, 0, 0, :, rows] = (contract(keys, grad_scores, 1, 0) * scale).astype(BF16)
        key_sum[:, :count] += contract(queries, grad_scores, 1, 1)
        value_sum[:, :count] += contract(grad_out, probs.astype(BF16), 1, 1)
    out_ref[0, 1, 0] = (key_sum[...] * scale).astype(BF16)
    out_ref[0, 2, 0] = value_sum[...].astype(BF16)


def attend_forward(qkv):
    groups, _, heads, width, length = qkv.shape
    return pl.pallas_call(
        forward_kernel,
        grid=(groups, heads),
        in_specs=[pl.BlockSpec((1, 3, 1, width, length), lambda g, h: (g, 0, h, 0, 0))],
        out_specs=[
            pl.BlockSpec((1, 1, width, length), lambda g, h: (g, h, 0, 0)),
            pl.BlockSpec((1, 1, 1, length), lambda g, h: (g, h, 0, 0)),
        ],
        out_shape=[
            jax.ShapeDtypeStruct((groups, heads, width, length), BF16),
            jax.ShapeDtypeStruct((groups, heads, 1, length), F32),
        ],
        compiler_params=pltpu.CompilerParams(vmem_limit_bytes=32 * 1024 * 1024),
        cost_estimate=pl.CostEstimate(
            flops=4 * groups * heads * length * length * width,
            bytes_accessed=8 * groups * heads * length * width,
            transcendentals=groups * heads * length * length,
        ),
    )(qkv)


def attend_backward(qkv, log_sums, grad_out):
    groups, _, heads, width, length = qkv.shape
    return pl.pallas_call(
        backward_kernel,
        grid=(groups, heads),
        in_specs=[
            pl.BlockSpec((1, 3, 1, width, length), lambda g, h: (g, 0, h, 0, 0)),
            pl.BlockSpec((1, 1, 1, length), lambda g, h: (g, h, 0, 0)),
            pl.BlockSpec((1, 1, width, length), lambda g, h: (g, h, 0, 0)),
        ],
        out_specs=pl.BlockSpec((1, 3, 1, width, length), lambda g, h: (g, 0, h, 0, 0)),
        out_shape=jax.ShapeDtypeStruct(qkv.shape, BF16),
        scratch_shapes=[pltpu.VMEM((width, length), F32), pltpu.VMEM((width, length), F32)],
        compiler_params=pltpu.CompilerParams(vmem_limit_bytes=32 * 1024 * 1024),
        cost_estimate=pl.CostEstimate(
            flops=10 * groups * heads * length * length * width,
            bytes_accessed=14 * groups * heads * length * width,
            transcendentals=groups * heads * length * length,
        ),
    )(qkv, log_sums, grad_out)


def swap(values, axis_name, distance):
    size = lax.axis_size(axis_name)
    return lax.ppermute(values, axis_name, [(i, i ^ distance) for i in range(size)])


def bit_of(axis_name, bit):
    return lax.rem(lax.axis_index(axis_name) // (1 << bit), 2)


def row_major(values):
    return with_layout_constraint(values, Layout(tuple(range(values.ndim))))


def gather_open(values, bits):
    blocks, rows, columns = values.shape
    return values.reshape((blocks,) + (1,) * bits + (rows, columns))


def gather_steps(values, bits, order):
    for bit in order:
        other = swap(values, "dp", 1 << bit)
        low = bit_of("dp", bit) == 0
        values = jnp.concatenate(
            [jnp.where(low, values, other), jnp.where(low, other, values)], axis=bits - bit
        )
    return values


def gather_close(values):
    return values.reshape(values.shape[0], -1, values.shape[-1])


def scatter_open(values, bits):
    blocks, rows, columns = values.shape
    return row_major(values).reshape((blocks,) + (2,) * bits + (rows >> bits, columns))


def scatter_steps(values, bits, order):
    for bit in order:
        mine = bit_of("dp", bit)
        axis = bits - bit
        other = swap(
            lax.dynamic_index_in_dim(values, 1 - mine, axis, keepdims=True), "dp", 1 << bit
        )
        kept = lax.dynamic_index_in_dim(values, mine, axis, keepdims=True)
        values = (kept.astype(F32) + other.astype(F32)).astype(BF16)
    return values


def tie(*values):
    return lax.optimization_barrier(values)


def gather_blocks(shard, distances):
    return jnp.stack([shard if d == 0 else swap(shard, "tensor", d) for d in distances])


def scatter_blocks(values, distances):
    total = values[0].astype(F32)
    for index, distance in enumerate(distances):
        if distance:
            total = total + swap(values[index], "tensor", distance).astype(F32)
    return total


def reduce_all(values):
    for axis_name in ("dp", "tensor"):
        distance = 1
        while distance < lax.axis_size(axis_name):
            values = values + swap(values, axis_name, distance)
            distance *= 2
    return values


def on_device(
    tokens,
    cotangent,
    w_qkv,
    w_out,
    w_up,
    w_down,
    vectors,
    m_qkv,
    v_qkv,
    m_out,
    v_out,
    m_up,
    v_up,
    m_down,
    v_down,
    m_vec,
    v_vec,
):
    width = tokens.shape[1]
    rows = tokens.shape[0]
    head_cols = w_qkv.shape[2]
    unit_cols = w_up.shape[1]
    own_rows = w_up.shape[0]
    n_tensor = lax.axis_size("tensor")
    bits = lax.axis_size("dp").bit_length() - 1
    outer = list(range(1, bits))
    near, far = outer, outer[::-1]
    rank = lax.axis_index("tensor")
    every = list(range(n_tensor))
    owned = every[::2]

    def vector(index):
        return vectors[index * width : (index + 1) * width]

    def ranked(first, count, distances):
        return jnp.stack(
            [
                lax.dynamic_slice_in_dim(vectors, first + (rank ^ d) * count, count)
                for d in distances
            ]
        )

    token_rows = tokens.astype(F32)
    cot_rows = cotangent.astype(F32)
    normed_one, norm_one_pull = jax.vjp(layer_norm, token_rows, vector(0), vector(1))
    normed_one = normed_one.astype(BF16)
    normed_other = swap(normed_one, "tensor", 1)
    half = lax.rem(rank, 2)
    first_half = half == 0
    normed_pair = jnp.concatenate(
        [
            jnp.where(first_half, normed_one, normed_other),
            jnp.where(first_half, normed_other, normed_one),
        ]
    )

    def exchange(values, axis):
        kept = lax.dynamic_slice_in_dim(values, half * rows, rows, axis)
        given = lax.dynamic_slice_in_dim(values, (1 - half) * rows, rows, axis)
        return kept, swap(given, "tensor", 1)

    qkv_shard = row_major(w_qkv.astype(BF16).transpose(1, 0, 2).reshape(own_rows, 3 * head_cols))
    up_out_shard = row_major(jnp.concatenate([w_up.astype(BF16), w_out.astype(BF16).T], axis=1))
    down_shard = row_major(w_down.astype(BF16).T)
    qkv_parts = gather_blocks(qkv_shard, owned)
    qkv_full = gather_close(
        jnp.concatenate(
            [
                gather_steps(gather_open(qkv_parts[:1], bits), bits, near + [0]),
                gather_steps(gather_open(qkv_parts[1:], bits), bits, far + [0]),
            ]
        )
    )
    up_out = gather_open(gather_blocks(up_out_shard, every), bits)
    down_full = gather_open(gather_blocks(down_shard, every), bits)
    qkv_full, up_out, down_full = tie(qkv_full, up_out, down_full)
    up_out = gather_steps(up_out, bits, near[:1])
    down_full = gather_steps(down_full, bits, far[:1])

    query_bias = ranked(6 * width, head_cols, owned)
    value_bias = ranked(7 * width, head_cols, owned)
    biases = jnp.concatenate([query_bias, jnp.zeros_like(query_bias), value_bias], axis=1)
    projected = jnp.einsum("jde,nd->jen", qkv_full, normed_pair, preferred_element_type=F32)
    projected = (projected + biases[:, :, None]).astype(BF16)
    projected, up_out, down_full = tie(projected, up_out, down_full)
    up_out = gather_steps(up_out, bits, near[1:])
    down_full = gather_steps(down_full, bits, far[1:])
    heads = head_cols // HEAD
    split = projected.reshape(len(owned), 3, heads, HEAD, 2 * rows)
    attended, log_sums = attend_forward(split)
    attended = attended.reshape(len(owned), head_cols, 2 * rows)
    attended, up_out, down_full = tie(attended, up_out, down_full)
    up_out = gather_close(gather_steps(up_out, bits, [0]))
    down_full = gather_close(gather_steps(down_full, bits, [0]))
    up_full, out_full = up_out[:, :, :unit_cols], up_out[:, :, unit_cols:]
    attended_own, attended_got = exchange(attended, 2)
    attended_all = jnp.stack([attended_own, attended_got], axis=1).reshape(
        n_tensor, head_cols, rows
    )
    branch = jnp.einsum("jen,jde->nd", attended_all, out_full, preferred_element_type=F32)
    hidden = token_rows + branch + vector(4)
    normed_two, norm_two_pull = jax.vjp(layer_norm, hidden, vector(2), vector(3))
    normed_two, down_full = tie(normed_two.astype(BF16), down_full)
    up_bias = ranked(8 * width, unit_cols, every)
    pre_act = (
        jnp.einsum("nd,jdf->jnf", normed_two, up_full, preferred_element_type=F32)
        + up_bias[:, None, :]
    )
    active, gelu_pull = jax.vjp(jax.nn.gelu, pre_act)
    active = active.astype(BF16)
    output = (
        hidden
        + jnp.einsum("jnf,jdf->nd", active, down_full, preferred_element_type=F32)
        + vector(5)
    )
    grad_active = jnp.einsum("nd,jdf->jnf", cotangent, down_full, preferred_element_type=F32)
    grad_pre = gelu_pull(grad_active)[0].astype(BF16)
    grad_down = jnp.einsum(
        "nd,jnf->jdf", cotangent, active, preferred_element_type=F32
    ).astype(BF16)
    grad_up = jnp.einsum("nd,jnf->jdf", normed_two, grad_pre, preferred_element_type=F32).astype(
        BF16
    )
    grad_normed_two = jnp.einsum("jnf,jdf->nd", grad_pre, up_full, preferred_element_type=F32)
    down_sum = scatter_steps(scatter_open(grad_down, bits), bits, [0])
    up_sum = scatter_steps(scatter_open(grad_up, bits), bits, [0])
    grad_normed_two, down_sum, up_sum = tie(grad_normed_two, down_sum, up_sum)
    down_sum = scatter_steps(down_sum, bits, near[:1])
    up_sum = scatter_steps(up_sum, bits, far[:1])
    up_sums = jnp.sum(grad_pre.astype(F32), axis=1)
    grad_from_norm, grad_gain_two, grad_shift_two = norm_two_pull(grad_normed_two)
    grad_hidden = cot_rows + grad_from_norm
    grad_low = grad_hidden.astype(BF16)
    grad_attended = jnp.einsum(
        "nd,jde->jen", grad_low, out_full, preferred_element_type=F32
    ).astype(BF16)
    grad_pairs = grad_attended.reshape(len(owned), 2, head_cols, rows)
    grad_other = swap(grad_pairs[:, 1], "tensor", 1)
    grad_own = grad_pairs[:, 0]
    grad_heads = jnp.concatenate(
        [
            jnp.where(first_half, grad_own, grad_other),
            jnp.where(first_half, grad_other, grad_own),
        ],
        axis=2,
    )
    grad_out_w = jnp.einsum(
        "nd,jen->jde", grad_low, attended_all, preferred_element_type=F32
    ).astype(BF16)
    grad_heads, down_sum, up_sum = tie(grad_heads, down_sum, up_sum)
    down_sum = scatter_steps(down_sum, bits, near[1:])
    up_sum = scatter_steps(up_sum, bits, far[1:])
    grad_split = attend_backward(
        split, log_sums, grad_heads.reshape(len(owned), heads, HEAD, 2 * rows)
    )
    grad_proj = grad_split.reshape(len(owned), 3 * head_cols, 2 * rows)
    grad_proj, down_sum, up_sum = tie(grad_proj, down_sum, up_sum)
    out_sum = scatter_steps(scatter_open(grad_out_w, bits), bits, [0] + near)

    def own_sum(values, distances):
        return scatter_blocks(values.reshape(values.shape[0], own_rows, -1), distances)

    grad_down_own = own_sum(down_sum, every)
    grad_up_own = own_sum(up_sum, every)
    grad_out_own = own_sum(out_sum, every)
    grad_normed_pair = jnp.einsum(
        "jen,jde->nd", grad_proj, qkv_full, preferred_element_type=F32
    ).astype(BF16)
    kept, given = exchange(grad_normed_pair, 0)
    grad_normed_one = kept.astype(F32) + given.astype(F32)
    grad_qkv_w = jnp.einsum(
        "nd,jen->jde", normed_pair, grad_proj, preferred_element_type=F32
    ).astype(BF16)
    qkv_sums = jnp.concatenate(
        [
            scatter_steps(scatter_open(grad_qkv_w[:1], bits), bits, [0] + near),
            scatter_steps(scatter_open(grad_qkv_w[1:], bits), bits, [0] + far),
        ]
    )
    grad_qkv_own = own_sum(qkv_sums, owned)
    grad_from_first, grad_gain_one, grad_shift_one = norm_one_pull(grad_normed_one)
    grad_tokens = grad_hidden + grad_from_first

    def placed(parts, count, full, distances):
        result = jnp.zeros((full,), F32)
        for index, distance in enumerate(distances):
            result = lax.dynamic_update_slice_in_dim(
                result, parts[index], (rank ^ distance) * count, 0
            )
        return result

    proj_sums = jnp.sum(grad_proj.astype(F32), axis=2)
    early = reduce_all(
        jnp.concatenate(
            [
                grad_gain_two,
                grad_shift_two,
                jnp.sum(grad_hidden, axis=0),
                jnp.sum(cot_rows, axis=0),
                placed(up_sums, unit_cols, n_tensor * unit_cols, every),
            ]
        )
    )
    late = reduce_all(
        jnp.concatenate(
            [
                grad_gain_one,
                grad_shift_one,
                placed(proj_sums[:, :head_cols], head_cols, width, owned),
                placed(proj_sums[:, 2 * head_cols :], head_cols, width, owned),
            ]
        )
    )
    vector_grad = jnp.concatenate(
        [
            late[: 2 * width],
            early[: 4 * width],
            late[2 * width :],
            early[4 * width :],
        ]
    )
    grad_qkv = grad_qkv_own.reshape(own_rows, 3, head_cols).transpose(1, 0, 2)
    qkv_new = adam_update(w_qkv, grad_qkv, m_qkv, v_qkv, D ** (-0.5), WEIGHT_DECAY)
    out_new = adam_update(w_out, grad_out_own.T, m_out, v_out, (D // 64) ** (-0.5), WEIGHT_DECAY)
    up_new = adam_update(w_up, grad_up_own, m_up, v_up, D ** (-0.5), WEIGHT_DECAY)
    down_new = adam_update(w_down, grad_down_own.T, m_down, v_down, FF ** (-0.5), WEIGHT_DECAY)
    vec_new = adam_update(vectors, vector_grad, m_vec, v_vec, VECTOR_RATE, 0.0)
    return (output.astype(BF16), grad_tokens, *qkv_new, *out_new, *up_new, *down_new, *vec_new)


def solution(mesh):
    return jax.shard_map(
        on_device,
        mesh=mesh,
        in_specs=(
            P(("dp", "tensor"), None),
            P(("dp", "tensor"), None),
            P(None, "dp", "tensor"),
            P("tensor", "dp"),
            P("dp", "tensor"),
            P("tensor", "dp"),
            P(),
            P(None, "dp", "tensor"),
            P(None, "dp", "tensor"),
            P("tensor", "dp"),
            P("tensor", "dp"),
            P("dp", "tensor"),
            P("dp", "tensor"),
            P("tensor", "dp"),
            P("tensor", "dp"),
            P(),
            P(),
        ),
        out_specs=(
            P(("dp", "tensor"), None),
            P(("dp", "tensor"), None),
            P(None, "dp", "tensor"),
            P(None, "dp", "tensor"),
            P(None, "dp", "tensor"),
            P("tensor", "dp"),
            P("tensor", "dp"),
            P("tensor", "dp"),
            P("dp", "tensor"),
            P("dp", "tensor"),
            P("dp", "tensor"),
            P("tensor", "dp"),
            P("tensor", "dp"),
            P("tensor", "dp"),
            P(),
            P(),
            P(),
        ),
        check_vma=False,
    )
```
